256 devices in a mesh: cuts: 8 (over x_lo, y), dev: 32 (over x_hi, z, core).
Axes of the slice: x: 4 (x_hi: 2, x_lo: 2; x = x_hi * 2 + x_lo), y: 4, z: 8, core: 2. Of those that a mesh axis runs over, the one named last changes fastest.
Arguments:
- gate_pre: bfloat16 [32768, 1024], P(('cuts', 'dev')), may hold values from -24 to 24
- up_pre: bfloat16 [32768, 1024], P(('cuts', 'dev')), may hold values from -6 to 6
- out_grad: bfloat16 [32768, 3584], P(('cuts', 'dev')), may hold values from -0.25 to 0.25
- route_weight: float32 [32768], P(('cuts', 'dev')), may hold values from 0.1 to 1
- row_token: int32 [32768], P(('cuts', 'dev')), may hold values from 0 to 127
- master: float32 [1024, 3584], P(('cuts', 'dev')), may hold values from -0.0625 to 0.0625
- moment: float32 [1024, 3584], P(('cuts', 'dev')), may hold values from -6 to 6
- second: float32 [1024, 3584], P(('cuts', 'dev')), may hold values from 0.1 to 4
Outputs:
- new_weight: bfloat16 [1024, 3584], replicated
- new_master: float32 [1024, 3584], P(('cuts', 'dev'))
- new_moment: float32 [1024, 3584], P(('cuts', 'dev'))
- new_second: float32 [1024, 3584], P(('cuts', 'dev'))
The draws below stay inside these ranges and needn't reach their ends.
Inputs may be any that keep to these rules, and one draw needn't show every extreme that they name: `row_token`: each entry names a row of out_grad in the same block of 128 rows as the entry itself.
All inputs are finite; a program needn't handle non-finite values.
Results may differ from the reference program's by a relative error of at most 0.01.
Values may be sent and summed in bfloat16 or wider, within the bound.
No kernel may reach another device: no remote copies, remote signals or barrier semaphores. Data moves between devices by JAX's collectives and lax.ppermute only.
A program may use at most 64 MiB of HBM per device.

```python
import math
import jax
import jax.numpy as jnp
from jax import lax

D = 3584
F = 1024
TOK_DEV = 128
STEP = 10
TOKENS = 32768
N_CUTS = 8
N_DEV = 32


def with_ends(entries, key, least, high):
    longest = entries.shape.index(max(entries.shape))
    spots = []
    for shift in (0, 1):
        where = [jax.random.randint(jax.random.fold_in(key, axis), (), 0, length) for axis, length in enumerate(entries.shape)]
        where[longest] = (where[longest] + shift) % entries.shape[longest]
        spots.append(tuple(where))
    return entries.at[spots[0]].set(least).at[spots[1]].set(high)


def strengthened(result, key, source, target, blocks, factor):
    def block_of(dim):
        return (jnp.arange(result.shape[dim]) // (result.shape[dim] // blocks)).reshape((-1,) + (1,) * (result.ndim - 1 - dim))

    near = jax.random.permutation(key, blocks)[block_of(target)]
    second = (block_of(target) + blocks // 2) % blocks
    return jnp.where((block_of(source) == near) | (block_of(source) == second), factor * result, result)


def levels(rng, extent, pieces, low, top_value):
    gain = 1.0
    for dim, blocks in pieces:
        steps = jax.random.uniform(jax.random.fold_in(jax.random.fold_in(rng, 6), dim), (blocks,), jnp.float32, low / len(pieces), top_value / len(pieces))
        gain = gain * jnp.repeat(jnp.exp(steps), extent[dim] // blocks).reshape((-1,) + (1,) * (len(extent) - 1 - dim))
    return gain


def gaussian(rng, dims, width, bound, split=(), held_as=jnp.bfloat16):
    values = jax.random.normal(rng, dims, jnp.float32) * width
    if len(split) > 0:
        values = levels(rng, dims, split, -0.22, 0.18) * values
    return jnp.clip(values, min=-bound, max=bound).astype(held_as)


def bell_draw_with(stream_key, extent, width, bound, cuts, heavy, held_as=jnp.bfloat16):
    values = width * jax.random.normal(stream_key, extent, jnp.float32)
    if cuts:
        values = values * levels(stream_key, extent, cuts, -0.22, 0.18)
    return jnp.clip(strengthened(values, jax.random.fold_in(stream_key, 3), *heavy), -bound, bound).astype(held_as)


def setup_inputs(seed: int = 0) -> dict:
    seeds = jax.random.split(jax.random.key(seed), 9)
    gate_pre = bell_draw_with(seeds[0], (TOKENS, F), 1.0, 24.0, ((0, 256),), (0, 1, 256, 6.0))
    up_pre = gaussian(seeds[1], (TOKENS, F), 1.0, 6.0, ((0, 256),))
    out_grad = gaussian(seeds[2], (TOKENS, D), (3.0 * TOKENS ** -0.5), 0.25, ((0, 256),))
    route_weight = jnp.clip(0.1 + 0.9 * jax.random.uniform(seeds[3], (TOKENS,), jnp.float32) ** levels(seeds[3], (TOKENS,), ((0, 256),), -0.2, 0.2), 0.1, 1.0)
    row_token = with_ends(jax.random.randint(seeds[4], (TOKENS,), 0, TOK_DEV), jax.random.fold_in(seeds[4], 1), 0, TOK_DEV - 1).astype(jnp.int32)
    master = gaussian(seeds[5], (F, D), 0.004, 0.0625, ((0, 256),), jnp.float32)
    moment = gaussian(seeds[6], (F, D), 0.5, 6.0, ((0, 256),), jnp.float32)
    second = jnp.clip(jnp.exp(math.log(4.0) - 3.6888794 * jax.random.uniform(seeds[7], (F, D), jnp.float32) ** levels(seeds[7], (F, D), ((0, 256),), -0.2, 0.2)), 0.1, 4.0)
    return dict(gate_pre=gate_pre, up_pre=up_pre, out_grad=out_grad, route_weight=route_weight, row_token=row_token, master=master, moment=moment, second=second)


def reference(gate_pre, up_pre, out_grad, route_weight, row_token, master, moment, second):
    hidden = (jax.nn.silu(gate_pre.astype(jnp.float32)) * up_pre.astype(jnp.float32)).astype(jnp.bfloat16)
    blocks = N_CUTS * N_DEV
    base = (jnp.arange(blocks, dtype=jnp.int32) * TOK_DEV)[:, None]
    index = (row_token.reshape(blocks, TOK_DEV).astype(jnp.int32) + base).reshape(-1)
    picked = jnp.take(out_grad, index, axis=0)
    scaled = (picked.astype(jnp.float32) * route_weight[:, None]).astype(jnp.bfloat16)
    hidden_blocks = hidden.reshape(blocks, TOK_DEV, F)
    scaled_blocks = scaled.reshape(blocks, TOK_DEV, D)

    def accumulate(total, pair):
        term = lax.dot_general(pair[0], pair[1], (((0,), (0,)), ((), ())), preferred_element_type=jnp.float32)
        return (total + term.astype(jnp.bfloat16).astype(jnp.float32), None)
    grad, unused = lax.scan(accumulate, jnp.zeros((F, D), jnp.float32), (hidden_blocks, scaled_blocks))
    new_moment = 0.9 * moment + 0.1 * grad
    new_second = 0.95 * second + 0.05 * grad * grad
    first_hat = new_moment / (1.0 - 0.9 ** STEP)
    second_hat = new_second / (1.0 - 0.95 ** STEP)
    new_master = master - 0.001 * (first_hat / (jnp.sqrt(second_hat) + 1e-08) + 0.1 * master)
    return (new_master.astype(jnp.bfloat16), new_master, new_moment, new_second)
```

```python
import jax
import jax.numpy as jnp
from jax import lax
from jax.sharding import Mesh, PartitionSpec as P

STEP = 10

SIZES = (2, 4, 2, 8, 2)
NAMES = ("xlo", "y", "xhi", "z", "core")
PLANE = ("xlo", "y", "xhi")
N_PLANE = 16
N_Z = 8
SWAP = [(0, 1), (1, 0)]


def gather_tokens(out_grad, row_token):
    return jnp.take(out_grad, row_token, axis=0, mode="clip")


def shards(gate_pre, up_pre, out_grad, route_weight, row_token, master, moment, second):
    first_core = lax.axis_index("core") == 0
    width = out_grad.shape[1]
    half = width // 2

    def mine_and_theirs(whole):
        left, right = whole[..., :half], whole[..., half:]
        return jnp.where(first_core, left, right), jnp.where(first_core, right, left)

    def in_core_order(own, peer, axis):
        return jnp.where(
            first_core,
            jnp.concatenate([own, peer], axis),
            jnp.concatenate([peer, own], axis),
        )

    state = jnp.stack([master, moment, second])
    state_mine, state_theirs = mine_and_theirs(state)
    state_peer = lax.ppermute(state_theirs, "core", SWAP)
    state_chip = in_core_order(state_mine, state_peer, 1)

    hidden = (jax.nn.silu(gate_pre.astype(jnp.float32)) * up_pre.astype(jnp.float32)).astype(
        jnp.bfloat16
    )
    hidden_peer = lax.ppermute(hidden, "core", SWAP)
    picked = gather_tokens(out_grad, row_token)
    scaled = (picked.astype(jnp.float32) * route_weight[:, None]).astype(jnp.bfloat16)
    scaled_mine, scaled_theirs = mine_and_theirs(scaled)
    scaled_peer = lax.ppermute(scaled_theirs, "core", SWAP)

    term = lax.dot_general(
        jnp.concatenate([hidden, hidden_peer], 0),
        jnp.concatenate([scaled_mine, scaled_peer], 0),
        (((0,), (0,)), ((), ())),
        preferred_element_type=jnp.float32,
    ).astype(jnp.bfloat16)
    rows = term.shape[0]
    blocks = lax.all_to_all(term.reshape(N_PLANE, rows // N_PLANE, half), PLANE, 0, 0)
    plane_sum = jnp.sum(blocks.astype(jnp.float32), 0).astype(jnp.bfloat16)
    rows = plane_sum.shape[0]
    blocks = lax.all_to_all(plane_sum.reshape(N_Z, rows // N_Z, half), "z", 0, 0)
    grad = jnp.sum(blocks.astype(jnp.float32), 0)

    new_moment = 0.9 * state_chip[1] + 0.1 * grad
    new_second = 0.95 * state_chip[2] + 0.05 * grad * grad
    first_hat = new_moment / (1.0 - 0.9**STEP)
    second_hat = new_second / (1.0 - 0.95**STEP)
    new_master = state_chip[0] - 0.001 * (
        first_hat / (jnp.sqrt(second_hat) + 1e-08) + 0.1 * state_chip[0]
    )
    piece = new_master.astype(jnp.bfloat16)

    new_state = jnp.stack([new_master, new_moment, new_second])
    top, bottom = new_state[:, : master.shape[0]], new_state[:, master.shape[0] :]
    state_own = jnp.where(first_core, top, bottom)
    state_back = lax.ppermute(jnp.where(first_core, bottom, top), "core", SWAP)
    state_out = in_core_order(state_own, state_back, 2)

    along_z = lax.all_to_all(jnp.broadcast_to(piece, (N_Z,) + piece.shape), "z", 0, 0)
    along_z = along_z.reshape(-1, half)
    plane = lax.all_to_all(jnp.broadcast_to(along_z, (N_PLANE,) + along_z.shape), PLANE, 0, 0)
    plane = plane.reshape(-1, half)
    plane_peer = lax.ppermute(plane, "core", SWAP)
    new_weight = in_core_order(plane, plane_peer, 1)
    return (new_weight, state_out[0], state_out[1], state_out[2])


def solution(mesh):
    grid = Mesh(mesh.devices.reshape(SIZES), NAMES)
    rows = P(NAMES, None)
    in_specs = (rows, rows, rows, P(NAMES), P(NAMES), rows, rows, rows)
    out_specs = (P(), rows, rows, rows)
    return jax.shard_map(shards, mesh=grid, in_specs=in_specs, out_specs=out_specs, check_vma=False)
```

```python
import functools

import jax
import jax.numpy as jnp
from jax import lax
from jax.experimental import pallas as pl
from jax.experimental.pallas import tpu as pltpu
from jax.sharding import Mesh, PartitionSpec as P

STEP = 10

SIZES = (2, 4, 2, 8, 2)
NAMES = ("xlo", "y", "xhi", "z", "core")
N_X = N_Y = 4
N_Z = 8
BLOCK = 64
SWAP = [(0, 1), (1, 0)]
VMEM = 40 * 1024 * 1024


def along_x(value, shift):
    place = [(x % 2) * 2 + x // 2 for x in range(N_X)]
    pairs = [(place[x], place[(x + shift) % N_X]) for x in range(N_X)]
    return lax.ppermute(value, ("xlo", "xhi"), pairs)


def along_y(value, shift):
    return lax.ppermute(value, "y", [(y, (y + shift) % N_Y) for y in range(N_Y)])


def block_of(x, y):
    return (x % 2) * 8 + y * 2 + x // 2


def position():
    return 2 * lax.axis_index("xhi") + lax.axis_index("xlo"), lax.axis_index("y")


def terms_kernel(here, hidden, hidden_peer, scaled, scaled_peer, *refs):
    outs, turned = refs[:-1], refs[-1]
    tokens = hidden.shape[0]
    turned[:, :tokens] = hidden[...].T
    turned[:, tokens:] = hidden_peer[...].T
    both = jnp.concatenate([scaled[...], scaled_peer[...]], 0)
    width = both.shape[1] // 2
    x, y = here[0], here[1]

    def rows(dx, dy):
        start = block_of((x + dx) % N_X, (y + dy) % N_Y) * BLOCK
        return turned[pl.ds(pl.multiple_of(start, BLOCK), BLOCK), :]

    for side in range(2):
        columns = both[:, side * width : (side + 1) * width]
        for far in range(4):
            for near in range(4):
                lhs = rows(near, far) if side == 0 else rows(far, near)
                outs[4 * side + far][near * BLOCK : (near + 1) * BLOCK, :] = jnp.dot(
                    lhs, columns, preferred_element_type=jnp.float32
                ).astype(jnp.bfloat16)


def terms(here, hidden, hidden_peer, scaled, scaled_peer):
    width = scaled.shape[1] // 2
    tokens = hidden.shape[0]
    whole = pl.BlockSpec(memory_space=pltpu.VMEM)
    return pl.pallas_call(
        terms_kernel,
        out_shape=[jax.ShapeDtypeStruct((4 * BLOCK, width), jnp.bfloat16)] * 8,
        in_specs=[pl.BlockSpec(memory_space=pltpu.SMEM)] + [whole] * 4,
        out_specs=[whole] * 8,
        scratch_shapes=[pltpu.VMEM((hidden.shape[1], 2 * tokens), jnp.bfloat16)],
        compiler_params=pltpu.CompilerParams(vmem_limit_bytes=VMEM),
        cost_estimate=pl.CostEstimate(
            flops=2 * 2 * tokens * hidden.shape[1] * 2 * width,
            bytes_accessed=5_000_000,
            transcendentals=0,
        ),
    )(here, hidden, hidden_peer, scaled, scaled_peer)


def join_kernel(here, *refs):
    pieces, out, sems = refs[:16], refs[16], refs[17]
    width = pieces[0].shape[1]
    x, y, core = here[0], here[1], here[2]
    copies = []
    for owner in range(2):
        column = (core if owner == 0 else 1 - core) * (2 * width)
        for side in range(2):
            for far in range(4):
                piece = pieces[8 * owner + 4 * side + far]
                for near in range(4):
                    dx, dy = (near, far) if side == 0 else (far, near)
                    row = block_of((x + N_X - dx) % N_X, (y + N_Y - dy) % N_Y) * BLOCK
                    copy = pltpu.make_async_copy(
                        piece.at[pl.ds(near * BLOCK, BLOCK), :],
                        out.at[
                            pl.ds(pl.multiple_of(row, BLOCK), BLOCK),
                            pl.ds(pl.multiple_of(column + side * width, 128), width),
                        ],
                        sems.at[len(copies)],
                    )
                    copy.start()
                    copies.append(copy)
    for copy in copies:
        copy.wait()


def join(here, pieces):
    rows, width = pieces[0].shape
    size = rows * width * 16
    return pl.pallas_call(
        join_kernel,
        out_shape=jax.ShapeDtypeStruct((4 * rows, 4 * width), jnp.bfloat16),
        in_specs=[pl.BlockSpec(memory_space=pltpu.SMEM)] + [pl.BlockSpec(memory_space=pl.ANY)] * 16,
        out_specs=pl.BlockSpec(memory_space=pl.ANY),
        scratch_shapes=[pltpu.SemaphoreType.DMA((64,))],
        compiler_params=pltpu.CompilerParams(vmem_limit_bytes=VMEM),
        cost_estimate=pl.CostEstimate(flops=0, bytes_accessed=4 * size, transcendentals=0),
    )(here, *pieces)


def total(parts):
    return functools.reduce(lambda a, b: a + b, [part.astype(jnp.float32) for part in parts])


def shards(gate_pre, up_pre, out_grad, route_weight, row_token, master, moment, second):
    first_core = lax.axis_index("core") == 0
    here = jnp.stack([*position(), lax.axis_index("core")]).astype(jnp.int32)
    half = out_grad.shape[1] // 2
    quarter = half // 2

    def mine_and_theirs(whole):
        left, right = whole[..., :half], whole[..., half:]
        return jnp.where(first_core, left, right), jnp.where(first_core, right, left)

    def in_core_order(own, peer, axis):
        return jnp.where(
            first_core,
            jnp.concatenate([own, peer], axis),
            jnp.concatenate([peer, own], axis),
        )

    state = jnp.stack([master, moment, second])
    state_mine, state_theirs = mine_and_theirs(state)
    state_peer = lax.ppermute(state_theirs, "core", SWAP)
    state_chip = in_core_order(state_mine, state_peer, 1)

    hidden = (jax.nn.silu(gate_pre.astype(jnp.float32)) * up_pre.astype(jnp.float32)).astype(
        jnp.bfloat16
    )
    hidden_peer = lax.ppermute(hidden, "core", SWAP)
    picked = jnp.take(out_grad, row_token, axis=0, mode="clip")
    scaled = (picked.astype(jnp.float32) * route_weight[:, None]).astype(jnp.bfloat16)
    scaled_mine, scaled_theirs = mine_and_theirs(scaled)
    scaled_peer = lax.ppermute(scaled_theirs, "core", SWAP)

    blocks = terms(here, hidden, hidden_peer, scaled_mine, scaled_peer)
    first = [along_y(blocks[s], s) for s in (1, 2, 3)]
    other = [along_x(blocks[4 + s], s) for s in (1, 2, 3)]
    first, other = [blocks[0]] + first, [blocks[4]] + other

    def near(parts, s):
        return total([part[s * BLOCK : (s + 1) * BLOCK] for part in parts])

    first = [near(first, 0)] + [along_x(near(first, s).astype(jnp.bfloat16), s) for s in (1, 2, 3)]
    other = [near(other, 0)] + [along_y(near(other, s).astype(jnp.bfloat16), s) for s in (1, 2, 3)]
    plane_sum = jnp.concatenate([total(first), total(other)], 1).astype(jnp.bfloat16)
    parts = lax.all_to_all(plane_sum.reshape(N_Z, BLOCK // N_Z, half), "z", 0, 0)
    grad = jnp.sum(parts.astype(jnp.float32), 0)

    new_moment = 0.9 * state_chip[1] + 0.1 * grad
    new_second = 0.95 * state_chip[2] + 0.05 * grad * grad
    first_hat = new_moment / (1.0 - 0.9**STEP)
    second_hat = new_second / (1.0 - 0.95**STEP)
    new_master = state_chip[0] - 0.001 * (
        first_hat / (jnp.sqrt(second_hat) + 1e-08) + 0.1 * state_chip[0]
    )
    piece = new_master.astype(jnp.bfloat16)

    new_state = jnp.stack([new_master, new_moment, new_second])
    top, bottom = new_state[:, : master.shape[0]], new_state[:, master.shape[0] :]
    state_own = jnp.where(first_core, top, bottom)
    state_back = lax.ppermute(jnp.where(first_core, bottom, top), "core", SWAP)
    state_out = in_core_order(state_own, state_back, 2)

    column = lax.all_to_all(jnp.broadcast_to(piece, (N_Z,) + piece.shape), "z", 0, 0)
    column = column.reshape(BLOCK, half)
    first, other = column[:, :quarter], column[:, quarter:]
    first = jnp.concatenate([first] + [along_x(first, s) for s in (1, 2, 3)], 0)
    other = jnp.concatenate([other] + [along_y(other, s) for s in (1, 2, 3)], 0)
    pieces = [first] + [along_y(first, s) for s in (1, 2, 3)]
    pieces += [other] + [along_x(other, s) for s in (1, 2, 3)]
    pieces += [lax.ppermute(piece, "core", SWAP) for piece in pieces]
    return (join(here, pieces), state_out[0], state_out[1], state_out[2])


def solution(mesh):
    grid = Mesh(mesh.devices.reshape(SIZES), NAMES)
    rows = P(NAMES, None)
    in_specs = (rows, rows, rows, P(NAMES), P(NAMES), rows, rows, rows)
    out_specs = (P(), rows, rows, rows)
    return jax.shard_map(shards, mesh=grid, in_specs=in_specs, out_specs=out_specs, check_vma=False)
```

```python
import functools

import jax
import jax.numpy as jnp
from jax import lax
from jax.experimental import pallas as pl
from jax.experimental.pallas import tpu as pltpu
from jax.sharding import Mesh, PartitionSpec as P

STEP = 10

SIZES = (2, 4, 2, 8, 2)
NAMES = ("xlo", "y", "xhi", "z", "core")
N_X = N_Y = 4
N_Z = 8
BLOCK = 64
SWAP = [(0, 1), (1, 0)]
VMEM = 40 * 1024 * 1024


def along_x(value, shift):
    place = [(x % 2) * 2 + x // 2 for x in range(N_X)]
    pairs = [(place[x], place[(x + shift) % N_X]) for x in range(N_X)]
    return lax.ppermute(value, ("xlo", "xhi"), pairs)


def along_y(value, shift):
    return lax.ppermute(value, "y", [(y, (y + shift) % N_Y) for y in range(N_Y)])


def block_of(x, y):
    return (x % 2) * 8 + y * 2 + x // 2


def position():
    return 2 * lax.axis_index("xhi") + lax.axis_index("xlo"), lax.axis_index("y")


def terms_kernel(here, hidden, hidden_peer, scaled, scaled_peer, *refs):
    outs, turned = refs[:-1], refs[-1]
    tokens = hidden.shape[0]
    turned[:, :tokens] = hidden[...].T
    turned[:, tokens:] = hidden_peer[...].T
    both = jnp.concatenate([scaled[...], scaled_peer[...]], 0)
    width = both.shape[1] // 2
    x, y = here[0], here[1]

    def rows(dx, dy):
        start = block_of((x + dx) % N_X, (y + dy) % N_Y) * BLOCK
        return turned[pl.ds(pl.multiple_of(start, BLOCK), BLOCK), :]

    for side in range(2):
        columns = both[:, side * width : (side + 1) * width]
        for far in range(4):
            for near in range(4):
                lhs = rows(near, far) if side == 0 else rows(far, near)
                outs[4 * side + far][near * BLOCK : (near + 1) * BLOCK, :] = jnp.dot(
                    lhs, columns, preferred_element_type=jnp.float32
                ).astype(jnp.bfloat16)


def terms(here, hidden, hidden_peer, scaled, scaled_peer):
    width = scaled.shape[1] // 2
    tokens = hidden.shape[0]
    whole = pl.BlockSpec(memory_space=pltpu.VMEM)
    return pl.pallas_call(
        terms_kernel,
        out_shape=[jax.ShapeDtypeStruct((4 * BLOCK, width), jnp.bfloat16)] * 8,
        in_specs=[pl.BlockSpec(memory_space=pltpu.SMEM)] + [whole] * 4,
        out_specs=[whole] * 8,
        scratch_shapes=[pltpu.VMEM((hidden.shape[1], 2 * tokens), jnp.bfloat16)],
        compiler_params=pltpu.CompilerParams(vmem_limit_bytes=VMEM),
        cost_estimate=pl.CostEstimate(
            flops=2 * 2 * tokens * hidden.shape[1] * 2 * width,
            bytes_accessed=5_000_000,
            transcendentals=0,
        ),
    )(here, hidden, hidden_peer, scaled, scaled_peer)


def join_kernel(here, *refs):
    pieces, out, sems = refs[:8], refs[-2], refs[-1]
    width = pieces[0].shape[1]
    x, y, column = here[0], here[1], here[2]
    copies = []

    def copy(source, row, column):
        started = pltpu.make_async_copy(
            source,
            out.at[
                pl.ds(pl.multiple_of(row, BLOCK), BLOCK),
                pl.ds(pl.multiple_of(column, 128), width),
            ],
            sems.at[len(copies)],
        )
        started.start()
        copies.append(started)

    for far in range(4):
        for near in range(4):
            place = pl.ds(near * BLOCK, BLOCK)
            row = block_of((x + N_X - near) % N_X, (y + N_Y - far) % N_Y) * BLOCK
            copy(pieces[far].at[place, :], row, column)
            row = block_of((x + N_X - far) % N_X, (y + N_Y - near) % N_Y) * BLOCK
            copy(pieces[4 + far].at[place, :], row, column + width)
    for started in copies:
        started.wait()


def join(here, core, pieces, out=None):
    rows, width = pieces[0].shape
    size = rows * width * 16
    place = jnp.stack([here[0], here[1], core * (2 * width)])
    anywhere = pl.BlockSpec(memory_space=pl.ANY)
    begun = [] if out is None else [out]
    return pl.pallas_call(
        join_kernel,
        out_shape=jax.ShapeDtypeStruct((4 * rows, 4 * width), jnp.bfloat16),
        in_specs=[pl.BlockSpec(memory_space=pltpu.SMEM)] + [anywhere] * (8 + len(begun)),
        out_specs=anywhere,
        scratch_shapes=[pltpu.SemaphoreType.DMA((32,))],
        input_output_aliases={9: 0} if begun else {},
        compiler_params=pltpu.CompilerParams(vmem_limit_bytes=VMEM),
        cost_estimate=pl.CostEstimate(flops=0, bytes_accessed=2 * size, transcendentals=0),
    )(place, *pieces, *begun)


def together(*values):
    return lax.optimization_barrier(values)


def after(value, earlier):
    return lax.optimization_barrier((value, earlier))[0]


def total(parts):
    return functools.reduce(lambda a, b: a + b, [part.astype(jnp.float32) for part in parts])


def shards(gate_pre, up_pre, out_grad, route_weight, row_token, master, moment, second):
    first_core = lax.axis_index("core") == 0
    here = jnp.stack([*position(), lax.axis_index("core")]).astype(jnp.int32)
    half = out_grad.shape[1] // 2
    quarter = half // 2

    def mine_and_theirs(whole):
        left, right = whole[..., :half], whole[..., half:]
        return jnp.where(first_core, left, right), jnp.where(first_core, right, left)

    def in_core_order(own, peer, axis):
        return jnp.where(
            first_core,
            jnp.concatenate([own, peer], axis),
            jnp.concatenate([peer, own], axis),
        )

    state = jnp.stack([master, moment, second])
    state_mine, state_theirs = mine_and_theirs(state)
    state_peer = lax.ppermute(state_theirs, "core", SWAP)
    state_chip = in_core_order(state_mine, state_peer, 1)

    hidden = (jax.nn.silu(gate_pre.astype(jnp.float32)) * up_pre.astype(jnp.float32)).astype(
        jnp.bfloat16
    )
    hidden_peer = lax.ppermute(hidden, "core", SWAP)
    picked = jnp.take(out_grad, row_token, axis=0, mode="clip")
    scaled = (picked.astype(jnp.float32) * route_weight[:, None]).astype(jnp.bfloat16)
    scaled_mine, scaled_theirs = mine_and_theirs(scaled)
    scaled_peer = lax.ppermute(scaled_theirs, "core", SWAP)

    blocks = terms(here, hidden, hidden_peer, scaled_mine, scaled_peer)
    parts = together(
        *[along_y(blocks[s], s) for s in (1, 3)],
        *[along_x(blocks[4 + s], s) for s in (1, 3)],
        along_x(blocks[6], 2),
        along_y(blocks[2], 2),
    )
    first, other = [blocks[0], *parts[0:2], parts[5]], [blocks[4], *parts[2:4], parts[4]]

    def near(parts, s):
        return total([part[s * BLOCK : (s + 1) * BLOCK] for part in parts])

    parts = together(
        *[near(first, s).astype(jnp.bfloat16) for s in (1, 3, 2)],
        *[near(other, s).astype(jnp.bfloat16) for s in (1, 3, 2)],
        near(first, 0), near(other, 0),
    )
    parts = together(
        *[along_x(parts[k], s) for k, s in enumerate((1, 3, 2))],
        *[along_y(parts[3 + k], s) for k, s in enumerate((1, 3, 2))],
        *parts[6:],
    )
    first, other = [parts[6], *parts[:3]], [parts[7], *parts[3:6]]
    plane_sum = jnp.concatenate([total(first), total(other)], 1).astype(jnp.bfloat16)
    parts = lax.all_to_all(plane_sum.reshape(N_Z, BLOCK // N_Z, half), "z", 0, 0)
    grad = jnp.sum(parts.astype(jnp.float32), 0)

    new_moment = 0.9 * state_chip[1] + 0.1 * grad
    new_second = 0.95 * state_chip[2] + 0.05 * grad * grad
    first_hat = new_moment / (1.0 - 0.9**STEP)
    second_hat = new_second / (1.0 - 0.95**STEP)
    new_master = state_chip[0] - 0.001 * (
        first_hat / (jnp.sqrt(second_hat) + 1e-08) + 0.1 * state_chip[0]
    )
    piece = new_master.astype(jnp.bfloat16)

    new_state = jnp.stack([new_master, new_moment, new_second])
    top, bottom = new_state[:, : master.shape[0]], new_state[:, master.shape[0] :]
    state_own = jnp.where(first_core, top, bottom)
    state_back = lax.ppermute(jnp.where(first_core, bottom, top), "core", SWAP)
    state_out = in_core_order(state_own, state_back, 2)

    column = lax.all_to_all(jnp.broadcast_to(piece, (N_Z,) + piece.shape), "z", 0, 0)
    column = column.reshape(BLOCK, half)
    first, other = together(column[:, :quarter], column[:, quarter:])
    parts = together(
        *[along_x(first, s) for s in (1, 2, 3)], *[along_y(other, s) for s in (1, 2, 3)]
    )
    first = jnp.concatenate([first, *parts[:3]], 0)
    other = jnp.concatenate([other, *parts[3:]], 0)
    first, other = together(first, other)
    pieces = list(together(
        first, *[along_y(first, s) for s in (1, 2, 3)],
        other, *[along_x(other, s) for s in (1, 2, 3)],
    ))
    swapped = [lax.ppermute(piece, "core", SWAP) for piece in pieces]
    core = here[2]
    new_weight = join(here, 1 - core, swapped, join(here, core, pieces))
    return (new_weight, state_out[0], state_out[1], state_out[2])


def solution(mesh):
    grid = Mesh(mesh.devices.reshape(SIZES), NAMES)
    rows = P(NAMES, None)
    in_specs = (rows, rows, rows, P(NAMES), P(NAMES), rows, rows, rows)
    out_specs = (P(), rows, rows, rows)
    return jax.shard_map(shards, mesh=grid, in_specs=in_specs, out_specs=out_specs, check_vma=False)
```

```python
import functools

import jax
import jax.numpy as jnp
from jax import lax
from jax.experimental import pallas as pl
from jax.experimental.pallas import tpu as pltpu
from jax.sharding import Mesh, PartitionSpec as P

STEP = 10

SIZES = (2, 4, 2, 8, 2)
NAMES = ("xlo", "y", "xhi", "z", "core")
N = 4
N_Z = 8
BLOCK = 64
SWAP = [(0, 1), (1, 0)]
VMEM = 40 * 1024 * 1024


def in_plane(value, shift, first_axis):
    def index(x, y, core):
        return (((x % 2) * N + y) * 2 + x // 2) * 2 + core

    pairs = []
    for x in range(N):
        for y in range(N):
            for core in range(2):
                if (core == 0) == first_axis:
                    there = index(x, (y + shift) % N, core)
                else:
                    there = index((x + shift) % N, y, core)
                pairs.append((index(x, y, core), there))
    return lax.ppermute(value, ("xlo", "y", "xhi", "core"), pairs)


def far(value, shift):
    return in_plane(value, shift, True)


def near(value, shift):
    return in_plane(value, shift, False)


def swap(value):
    return lax.ppermute(value, "core", SWAP)


def block_row(here, core, far_step, near_step):
    dx = near_step + core * (far_step - near_step)
    dy = far_step + core * (near_step - far_step)
    x, y = (here[0] + dx) % N, (here[1] + dy) % N
    return pl.multiple_of(((x % 2) * 8 + y * 2 + x // 2) * BLOCK, BLOCK)


def terms_kernel(here, hidden, hidden_peer, scaled, scaled_peer, *refs):
    outs, turned = refs[:-1], refs[-1]
    tokens = hidden.shape[0]
    turned[:, :tokens] = hidden[...].T
    turned[:, tokens:] = hidden_peer[...].T
    columns = jnp.concatenate([scaled[...], scaled_peer[...]], 0)
    for f in range(N):
        rows = [turned[pl.ds(block_row(here, here[2], f, n), BLOCK), :] for n in range(N)]
        outs[f][...] = jnp.dot(
            jnp.concatenate(rows, 0), columns, preferred_element_type=jnp.float32
        ).astype(jnp.bfloat16)


def terms(here, hidden, hidden_peer, scaled, scaled_peer):
    tokens, width = scaled.shape
    whole = pl.BlockSpec(memory_space=pltpu.VMEM)
    return pl.pallas_call(
        terms_kernel,
        out_shape=[jax.ShapeDtypeStruct((N * BLOCK, width), jnp.bfloat16)] * N,
        in_specs=[pl.BlockSpec(memory_space=pltpu.SMEM)] + [whole] * 4,
        out_specs=[whole] * N,
        scratch_shapes=[pltpu.VMEM((hidden.shape[1], 2 * tokens), jnp.bfloat16)],
        compiler_params=pltpu.CompilerParams(vmem_limit_bytes=VMEM),
        cost_estimate=pl.CostEstimate(
            flops=2 * 2 * tokens * hidden.shape[1] * width,
            bytes_accessed=5_000_000,
            transcendentals=0,
        ),
    )(here, hidden, hidden_peer, scaled, scaled_peer)


def join_kernel(plan, here, *refs):
    pieces, out, sems = refs[: len(plan)], refs[-2], refs[-1]
    width = pieces[0].shape[1]
    copies = []
    for piece, (shift, begin, theirs) in zip(pieces, plan):
        core = 1 - here[2] if theirs else here[2]
        for n in range(piece.shape[0] // BLOCK):
            copy = pltpu.make_async_copy(
                piece.at[pl.ds(n * BLOCK, BLOCK), :],
                out.at[
                    pl.ds(block_row(here, core, N - shift, N - begin - n), BLOCK),
                    pl.ds(pl.multiple_of(core * width, 128), width),
                ],
                sems.at[len(copies)],
            )
            copy.start()
            copies.append(copy)
    for copy in copies:
        copy.wait()


def join(here, items, out=None):
    pieces = [item[0] for item in items]
    width = pieces[0].shape[1]
    blocks = sum(piece.shape[0] for piece in pieces) // BLOCK
    anywhere = pl.BlockSpec(memory_space=pl.ANY)
    begun = [] if out is None else [out]
    return pl.pallas_call(
        functools.partial(join_kernel, tuple(item[1:] for item in items)),
        out_shape=jax.ShapeDtypeStruct((N * N * BLOCK, 2 * width), jnp.bfloat16),
        in_specs=[pl.BlockSpec(memory_space=pltpu.SMEM)]
        + [pl.BlockSpec(memory_space=pltpu.VMEM)] * len(pieces)
        + [anywhere] * len(begun),
        out_specs=anywhere,
        scratch_shapes=[pltpu.SemaphoreType.DMA((blocks,))],
        input_output_aliases={len(pieces) + 1: 0} if begun else {},
        compiler_params=pltpu.CompilerParams(vmem_limit_bytes=VMEM),
        cost_estimate=pl.CostEstimate(
            flops=0, bytes_accessed=4 * blocks * BLOCK * width, transcendentals=0
        ),
    )(here, *pieces, *begun)


def together(*values):
    return lax.optimization_barrier(values)


def after(value, earlier):
    return lax.optimization_barrier((value, earlier))[0]


def total(parts):
    return functools.reduce(lambda a, b: a + b, [part.astype(jnp.float32) for part in parts])


def shards(gate_pre, up_pre, out_grad, route_weight, row_token, master, moment, second):
    core = lax.axis_index("core")
    first_core = core == 0
    here = jnp.stack([2 * lax.axis_index("xhi") + lax.axis_index("xlo"), lax.axis_index("y"), core])
    here = here.astype(jnp.int32)
    half = out_grad.shape[1] // 2

    def mine_and_theirs(whole):
        left, right = whole[..., :half], whole[..., half:]
        return jnp.where(first_core, left, right), jnp.where(first_core, right, left)

    def in_core_order(own, peer, axis):
        return jnp.where(
            first_core,
            jnp.concatenate([own, peer], axis),
            jnp.concatenate([peer, own], axis),
        )

    state = jnp.stack([master, moment, second])
    state_mine, state_theirs = mine_and_theirs(state)

    hidden = (jax.nn.silu(gate_pre.astype(jnp.float32)) * up_pre.astype(jnp.float32)).astype(
        jnp.bfloat16
    )
    named = row_token[:, None] == jnp.arange(out_grad.shape[0], dtype=jnp.int32)[None, :]
    picked = jnp.dot(named.astype(jnp.bfloat16), out_grad, preferred_element_type=jnp.float32)
    scaled = (picked * route_weight[:, None]).astype(jnp.bfloat16)
    scaled_mine, scaled_theirs = mine_and_theirs(scaled)

    blocks = terms(here, hidden, swap(hidden), scaled_mine, swap(scaled_theirs))
    *parts, state_peer = together(*[far(blocks[s], s) for s in (2, 1, 3)], swap(state_theirs))
    parts = [blocks[0], *parts]
    state_chip = in_core_order(state_mine, state_peer, 1)
    sums = [total([part[s * BLOCK : (s + 1) * BLOCK] for part in parts]) for s in range(N)]
    sums = together(sums[0], *[sums[s].astype(jnp.bfloat16) for s in (2, 1, 3)])
    parts = [sums[0], *together(*[near(value, s) for value, s in zip(sums[1:], (2, 1, 3))])]
    plane_sum = total(parts).astype(jnp.bfloat16)
    parts = lax.all_to_all(plane_sum.reshape(N_Z, BLOCK // N_Z, half), "z", 0, 0)
    grad = jnp.sum(parts.astype(jnp.float32), 0)

    new_moment = 0.9 * state_chip[1] + 0.1 * grad
    new_second = 0.95 * state_chip[2] + 0.05 * grad * grad
    first_hat = new_moment / (1.0 - 0.9**STEP)
    second_hat = new_second / (1.0 - 0.95**STEP)
    new_master = state_chip[0] - 0.001 * (
        first_hat / (jnp.sqrt(second_hat) + 1e-08) + 0.1 * state_chip[0]
    )
    piece = new_master.astype(jnp.bfloat16)

    new_state = jnp.stack([new_master, new_moment, new_second])
    top, bottom = new_state[:, : master.shape[0]], new_state[:, master.shape[0] :]
    state_own = jnp.where(first_core, top, bottom)
    state_out = in_core_order(state_own, swap(jnp.where(first_core, bottom, top)), 2)

    column = lax.all_to_all(jnp.broadcast_to(piece, (N_Z,) + piece.shape), "z", 0, 0)
    column = together(column.reshape(BLOCK, half))[0]
    parts = together(*[near(column, s) for s in (1, 2, 3)])
    (plane,) = together(jnp.concatenate([column, *parts], 0))
    one, three, peer, *state_out = together(
        far(plane, 1), far(plane, 3), swap(plane), *[state_out[k] for k in range(3)]
    )
    middle = plane.shape[0] // 2
    two_a, two_b, one_peer, three_peer, weight = together(
        far(one[:middle], 1),
        far(three[middle:], 3),
        swap(one),
        swap(three),
        join(here, [(plane, 0, 0, 0), (one, 1, 0, 0), (three, 3, 0, 0), (peer, 0, 0, 1)]),
    )
    items = [(two_a, 2, 0, 0), (two_b, 2, 2, 0), (one_peer, 1, 0, 1), (three_peer, 3, 0, 1)]
    items += [(swap(two_a), 2, 0, 1), (swap(two_b), 2, 2, 1)]
    weight = join(here, items, weight)
    return (weight, state_out[0], state_out[1], state_out[2])


def solution(mesh):
    grid = Mesh(mesh.devices.reshape(SIZES), NAMES)
    rows = P(NAMES, None)
    in_specs = (rows, rows, rows, P(NAMES), P(NAMES), rows, rows, rows)
    out_specs = (P(), rows, rows, rows)
    return jax.shard_map(shards, mesh=grid, in_specs=in_specs, out_specs=out_specs, check_vma=False)
```

```python
import functools

import jax
import jax.numpy as jnp
from jax import lax
from jax.experimental import pallas as pl
from jax.experimental.pallas import tpu as pltpu
from jax.sharding import Mesh, PartitionSpec as P

STEP = 10

SIZES = (2, 4, 2, 8, 2)
NAMES = ("xlo", "y", "xhi", "z", "core")
N = 4
N_Z = 8
BLOCK = 64
SWAP = [(0, 1), (1, 0)]
VMEM = 40 * 1024 * 1024


def in_plane(value, shift, first_axis):
    def index(x, y, core):
        return (((x % 2) * N + y) * 2 + x // 2) * 2 + core

    pairs = []
    for x in range(N):
        for y in range(N):
            for core in range(2):
                if (core == 0) == first_axis:
                    there = index(x, y ^ shift, core)
                else:
                    there = index(x ^ shift, y, core)
                pairs.append((index(x, y, core), there))
    return lax.ppermute(value, ("xlo", "y", "xhi", "core"), pairs)


def far(value, shift):
    return in_plane(value, shift, True)


def near(value, shift):
    return in_plane(value, shift, False)


def swap(value):
    return lax.ppermute(value, "core", SWAP)


def block_row(here, core, far_step, near_step):
    dx = near_step + core * (far_step - near_step)
    dy = far_step + core * (near_step - far_step)
    x, y = here[0] ^ dx, here[1] ^ dy
    return pl.multiple_of(((x % 2) * 8 + y * 2 + x // 2) * BLOCK, BLOCK)


def terms_kernel(here, hidden, hidden_peer, scaled, scaled_peer, *refs):
    outs, turned = refs[:-1], refs[-1]
    tokens = hidden.shape[0]
    turned[:, :tokens] = hidden[...].T
    turned[:, tokens:] = hidden_peer[...].T
    columns = jnp.concatenate([scaled[...], scaled_peer[...]], 0)
    for f in range(N):
        rows = [turned[pl.ds(block_row(here, here[2], f, n), BLOCK), :] for n in range(N)]
        outs[f][...] = jnp.dot(
            jnp.concatenate(rows, 0), columns, preferred_element_type=jnp.float32
        ).astype(jnp.bfloat16)


def terms(here, hidden, hidden_peer, scaled, scaled_peer):
    tokens, width = scaled.shape
    whole = pl.BlockSpec(memory_space=pltpu.VMEM)
    return pl.pallas_call(
        terms_kernel,
        out_shape=[jax.ShapeDtypeStruct((N * BLOCK, width), jnp.bfloat16)] * N,
        in_specs=[pl.BlockSpec(memory_space=pltpu.SMEM)] + [whole] * 4,
        out_specs=[whole] * N,
        scratch_shapes=[pltpu.VMEM((hidden.shape[1], 2 * tokens), jnp.bfloat16)],
        compiler_params=pltpu.CompilerParams(vmem_limit_bytes=VMEM),
        cost_estimate=pl.CostEstimate(
            flops=2 * 2 * tokens * hidden.shape[1] * width,
            bytes_accessed=5_000_000,
            transcendentals=0,
        ),
    )(here, hidden, hidden_peer, scaled, scaled_peer)


def join_kernel(plan, here, *refs):
    pieces, out, sems = refs[: len(plan)], refs[-2], refs[-1]
    width = pieces[0].shape[1]
    copies = []
    for piece, (shift, begin, theirs) in zip(pieces, plan):
        core = 1 - here[2] if theirs else here[2]
        for n in range(piece.shape[0] // BLOCK):
            copy = pltpu.make_async_copy(
                piece.at[pl.ds(n * BLOCK, BLOCK), :],
                out.at[
                    pl.ds(block_row(here, core, shift, begin + n), BLOCK),
                    pl.ds(pl.multiple_of(core * width, 128), width),
                ],
                sems.at[len(copies)],
            )
            copy.start()
            copies.append(copy)
    for copy in copies:
        copy.wait()


def join(here, items, out=None):
    pieces = [item[0] for item in items]
    width = pieces[0].shape[1]
    blocks = sum(piece.shape[0] for piece in pieces) // BLOCK
    anywhere = pl.BlockSpec(memory_space=pl.ANY)
    begun = [] if out is None else [out]
    return pl.pallas_call(
        functools.partial(join_kernel, tuple(item[1:] for item in items)),
        out_shape=jax.ShapeDtypeStruct((N * N * BLOCK, 2 * width), jnp.bfloat16),
        in_specs=[pl.BlockSpec(memory_space=pltpu.SMEM)]
        + [pl.BlockSpec(memory_space=pltpu.VMEM)] * len(pieces)
        + [anywhere] * len(begun),
        out_specs=anywhere,
        scratch_shapes=[pltpu.SemaphoreType.DMA((blocks,))],
        input_output_aliases={len(pieces) + 1: 0} if begun else {},
        compiler_params=pltpu.CompilerParams(vmem_limit_bytes=VMEM),
        cost_estimate=pl.CostEstimate(
            flops=0, bytes_accessed=4 * blocks * BLOCK * width, transcendentals=0
        ),
    )(here, *pieces, *begun)


def together(*values):
    return lax.optimization_barrier(values)


def after(value, earlier):
    return lax.optimization_barrier((value, earlier))[0]


def total(parts):
    return functools.reduce(lambda a, b: a + b, [part.astype(jnp.float32) for part in parts])


def shards(gate_pre, up_pre, out_grad, route_weight, row_token, master, moment, second):
    core = lax.axis_index("core")
    first_core = core == 0
    here = jnp.stack([2 * lax.axis_index("xhi") + lax.axis_index("xlo"), lax.axis_index("y"), core])
    here = here.astype(jnp.int32)
    half = out_grad.shape[1] // 2

    def mine_and_theirs(whole):
        left, right = whole[..., :half], whole[..., half:]
        return jnp.where(first_core, left, right), jnp.where(first_core, right, left)

    def in_core_order(own, peer, axis):
        return jnp.where(
            first_core,
            jnp.concatenate([own, peer], axis),
            jnp.concatenate([peer, own], axis),
        )

    state = jnp.stack([master, moment, second])
    state_mine, state_theirs = mine_and_theirs(state)

    hidden = (jax.nn.silu(gate_pre.astype(jnp.float32)) * up_pre.astype(jnp.float32)).astype(
        jnp.bfloat16
    )
    named = row_token[:, None] == jnp.arange(out_grad.shape[0], dtype=jnp.int32)[None, :]
    picked = jnp.dot(named.astype(jnp.bfloat16), out_grad, preferred_element_type=jnp.float32)
    scaled = (picked * route_weight[:, None]).astype(jnp.bfloat16)
    scaled_mine, scaled_theirs = mine_and_theirs(scaled)

    blocks = terms(here, hidden, swap(hidden), scaled_mine, swap(scaled_theirs))
    *parts, state_peer = together(*[far(blocks[s], s) for s in (2, 1, 3)], swap(state_theirs))
    parts = [blocks[0], *parts]
    state_chip = in_core_order(state_mine, state_peer, 1)
    sums = [total([part[s * BLOCK : (s + 1) * BLOCK] for part in parts]) for s in range(N)]
    sums = together(sums[0], *[sums[s].astype(jnp.bfloat16) for s in (2, 1, 3)])
    parts = [sums[0], *together(*[near(value, s) for value, s in zip(sums[1:], (2, 1, 3))])]
    plane_sum = total(parts).astype(jnp.bfloat16)
    parts = lax.all_to_all(plane_sum.reshape(N_Z, BLOCK // N_Z, half), "z", 0, 0)
    grad = jnp.sum(parts.astype(jnp.float32), 0)

    new_moment = 0.9 * state_chip[1] + 0.1 * grad
    new_second = 0.95 * state_chip[2] + 0.05 * grad * grad
    first_hat = new_moment / (1.0 - 0.9**STEP)
    second_hat = new_second / (1.0 - 0.95**STEP)
    new_master = state_chip[0] - 0.001 * (
        first_hat / (jnp.sqrt(second_hat) + 1e-08) + 0.1 * state_chip[0]
    )
    piece = new_master.astype(jnp.bfloat16)

    new_state = jnp.stack([new_master, new_moment, new_second])
    top, bottom = new_state[:, : master.shape[0]], new_state[:, master.shape[0] :]
    state_own = jnp.where(first_core, top, bottom)
    state_out = in_core_order(state_own, swap(jnp.where(first_core, bottom, top)), 2)

    column = lax.all_to_all(jnp.broadcast_to(piece, (N_Z,) + piece.shape), "z", 0, 0)
    column = together(column.reshape(BLOCK, half))[0]
    parts = together(*[near(column, s) for s in (1, 2, 3)])
    (plane,) = together(jnp.concatenate([column, *parts], 0))
    two = far(plane, 2)
    one, three, peer, *state_out = together(
        far(plane, 1), far(plane, 3), swap(plane), *[state_out[k] for k in range(3)]
    )
    items = [(plane, 0, 0, 0), (one, 1, 0, 0), (three, 3, 0, 0), (peer, 0, 0, 1)]
    two, one_peer, three_peer, weight = together(two, swap(one), swap(three), join(here, items))
    items = [(two, 2, 0, 0), (one_peer, 1, 0, 1), (three_peer, 3, 0, 1)]
    two_peer, weight = together(swap(two), join(here, items, weight))
    weight = join(here, [(two_peer, 2, 0, 1)], weight)
    return (weight, state_out[0], state_out[1], state_out[2])


def solution(mesh):
    grid = Mesh(mesh.devices.reshape(SIZES), NAMES)
    rows = P(NAMES, None)
    in_specs = (rows, rows, rows, P(NAMES), P(NAMES), rows, rows, rows)
    out_specs = (P(), rows, rows, rows)
    return jax.shard_map(shards, mesh=grid, in_specs=in_specs, out_specs=out_specs, check_vma=False)
```

```python
import functools

import jax
import jax.numpy as jnp
from jax import lax
from jax.experimental import pallas as pl
from jax.experimental.pallas import tpu as pltpu
from jax.sharding import Mesh, PartitionSpec as P

STEP = 10

SIZES = (2, 4, 2, 8, 2)
NAMES = ("xlo", "y", "xhi", "z", "core")
N = 4
N_Z = 8
BLOCK = 64
SWAP = [(0, 1), (1, 0)]
VMEM = 40 * 1024 * 1024


def in_plane(value, shift, first_axis):
    def index(x, y, core):
        return (((x % 2) * N + y) * 2 + x // 2) * 2 + core

    pairs = []
    for x in range(N):
        for y in range(N):
            for core in range(2):
                if (core == 0) == first_axis:
                    there = index(x, y ^ shift, core)
                else:
                    there = index(x ^ shift, y, core)
                pairs.append((index(x, y, core), there))
    return lax.ppermute(value, ("xlo", "y", "xhi", "core"), pairs)


def far(value, shift):
    return in_plane(value, shift, True)


def near(value, shift):
    return in_plane(value, shift, False)


def swap(value):
    return lax.ppermute(value, "core", SWAP)


def block_row(here, core, far_step, near_step):
    dx = near_step + core * (far_step - near_step)
    dy = far_step + core * (near_step - far_step)
    x, y = here[0] ^ dx, here[1] ^ dy
    return pl.multiple_of(((x % 2) * 8 + y * 2 + x // 2) * BLOCK, BLOCK)


def terms_kernel(here, hidden, hidden_peer, scaled, scaled_peer, *refs):
    outs, turned = refs[:-1], refs[-1]
    tokens = hidden.shape[0]
    turned[:, :tokens] = hidden[...].T
    turned[:, tokens:] = hidden_peer[...].T
    columns = jnp.concatenate([scaled[...], scaled_peer[...]], 0)
    for f in range(N):
        rows = [turned[pl.ds(block_row(here, here[2], f, n), BLOCK), :] for n in range(N)]
        block = jnp.dot(jnp.concatenate(rows, 0), columns, preferred_element_type=jnp.float32)
        outs[f][...] = block[: 2 * BLOCK].astype(jnp.bfloat16)
        outs[N + f][...] = block[2 * BLOCK :].astype(jnp.bfloat16)


def terms(here, hidden, hidden_peer, scaled, scaled_peer):
    tokens, width = scaled.shape
    whole = pl.BlockSpec(memory_space=pltpu.VMEM)
    return pl.pallas_call(
        terms_kernel,
        out_shape=[jax.ShapeDtypeStruct((2 * BLOCK, width), jnp.bfloat16)] * (2 * N),
        in_specs=[pl.BlockSpec(memory_space=pltpu.SMEM)] + [whole] * 4,
        out_specs=[whole] * (2 * N),
        scratch_shapes=[pltpu.VMEM((hidden.shape[1], 2 * tokens), jnp.bfloat16)],
        compiler_params=pltpu.CompilerParams(vmem_limit_bytes=VMEM),
        cost_estimate=pl.CostEstimate(
            flops=2 * 2 * tokens * hidden.shape[1] * width,
            bytes_accessed=5_000_000,
            transcendentals=0,
        ),
    )(here, hidden, hidden_peer, scaled, scaled_peer)


def join_kernel(plan, here, *refs):
    pieces, out, sems = refs[: len(plan)], refs[-2], refs[-1]
    width = pieces[0].shape[1]
    copies = []
    for piece, (shift, begin, theirs) in zip(pieces, plan):
        core = 1 - here[2] if theirs else here[2]
        for n in range(piece.shape[0] // BLOCK):
            copy = pltpu.make_async_copy(
                piece.at[pl.ds(n * BLOCK, BLOCK), :],
                out.at[
                    pl.ds(block_row(here, core, shift, begin + n), BLOCK),
                    pl.ds(pl.multiple_of(core * width, 128), width),
                ],
                sems.at[len(copies)],
            )
            copy.start()
            copies.append(copy)
    for copy in copies:
        copy.wait()


def join(here, items, out=None):
    pieces = [item[0] for item in items]
    width = pieces[0].shape[1]
    blocks = sum(piece.shape[0] for piece in pieces) // BLOCK
    anywhere = pl.BlockSpec(memory_space=pl.ANY)
    begun = [] if out is None else [out]
    return pl.pallas_call(
        functools.partial(join_kernel, tuple(item[1:] for item in items)),
        out_shape=jax.ShapeDtypeStruct((N * N * BLOCK, 2 * width), jnp.bfloat16),
        in_specs=[pl.BlockSpec(memory_space=pltpu.SMEM)]
        + [pl.BlockSpec(memory_space=pltpu.VMEM)] * len(pieces)
        + [anywhere] * len(begun),
        out_specs=anywhere,
        scratch_shapes=[pltpu.SemaphoreType.DMA((blocks,))],
        input_output_aliases={len(pieces) + 1: 0} if begun else {},
        compiler_params=pltpu.CompilerParams(vmem_limit_bytes=VMEM),
        cost_estimate=pl.CostEstimate(
            flops=0, bytes_accessed=4 * blocks * BLOCK * width, transcendentals=0
        ),
    )(here, *pieces, *begun)


def together(*values):
    return lax.optimization_barrier(values)


def after(value, earlier):
    return lax.optimization_barrier((value, earlier))[0]


def total(parts):
    return functools.reduce(lambda a, b: a + b, [part.astype(jnp.float32) for part in parts])


def shards(gate_pre, up_pre, out_grad, route_weight, row_token, master, moment, second):
    core = lax.axis_index("core")
    first_core = core == 0
    here = jnp.stack([2 * lax.axis_index("xhi") + lax.axis_index("xlo"), lax.axis_index("y"), core])
    here = here.astype(jnp.int32)
    half = out_grad.shape[1] // 2

    def mine_and_theirs(whole):
        left, right = whole[..., :half], whole[..., half:]
        return jnp.where(first_core, left, right), jnp.where(first_core, right, left)

    def in_core_order(own, peer, axis):
        return jnp.where(
            first_core,
            jnp.concatenate([own, peer], axis),
            jnp.concatenate([peer, own], axis),
        )

    state = jnp.stack([master, moment, second])
    state_mine, state_theirs = mine_and_theirs(state)

    hidden = (jax.nn.silu(gate_pre.astype(jnp.float32)) * up_pre.astype(jnp.float32)).astype(
        jnp.bfloat16
    )
    named = row_token[:, None] == jnp.arange(out_grad.shape[0], dtype=jnp.int32)[None, :]
    picked = jnp.dot(named.astype(jnp.bfloat16), out_grad, preferred_element_type=jnp.float32)
    scaled = (picked * route_weight[:, None]).astype(jnp.bfloat16)
    scaled_mine, scaled_theirs = mine_and_theirs(scaled)

    blocks = terms(here, hidden, swap(hidden), scaled_mine, swap(scaled_theirs))
    tops, bottoms = blocks[:N], blocks[N:]
    from_one, from_three = far(bottoms[1], 1), far(tops[3], 3)
    over_three, over_one = together(far(tops[2], 3), far(bottoms[2], 1))
    to_one, to_three = together(
        total([tops[1], over_three]).astype(jnp.bfloat16),
        total([bottoms[3], over_one]).astype(jnp.bfloat16),
    )
    from_one, from_three, both_one, both_three, state_peer = together(
        from_one, from_three, far(to_one, 1), far(to_three, 3), swap(state_theirs)
    )
    state_chip = in_core_order(state_mine, state_peer, 1)
    halves = [[tops[0], both_one, from_three], [bottoms[0], from_one, both_three]]
    sums = [
        total([part[s % 2 * BLOCK : (s % 2 + 1) * BLOCK] for part in halves[s // 2]]) for s in range(N)
    ]
    sums = together(sums[0], *[sums[s].astype(jnp.bfloat16) for s in (2, 1, 3)])
    parts = [sums[0], *together(*[near(value, s) for value, s in zip(sums[1:], (2, 1, 3))])]
    plane_sum = total(parts).astype(jnp.bfloat16)
    parts = lax.all_to_all(plane_sum.reshape(N_Z, BLOCK // N_Z, half), "z", 0, 0)
    grad = jnp.sum(parts.astype(jnp.float32), 0)

    new_moment = 0.9 * state_chip[1] + 0.1 * grad
    new_second = 0.95 * state_chip[2] + 0.05 * grad * grad
    first_hat = new_moment / (1.0 - 0.9**STEP)
    second_hat = new_second / (1.0 - 0.95**STEP)
    new_master = state_chip[0] - 0.001 * (
        first_hat / (jnp.sqrt(second_hat) + 1e-08) + 0.1 * state_chip[0]
    )
    piece = new_master.astype(jnp.bfloat16)

    new_state = jnp.stack([new_master, new_moment, new_second])
    top, bottom = new_state[:, : master.shape[0]], new_state[:, master.shape[0] :]
    state_own = jnp.where(first_core, top, bottom)
    state_out = in_core_order(state_own, swap(jnp.where(first_core, bottom, top)), 2)

    column = lax.all_to_all(jnp.broadcast_to(piece, (N_Z,) + piece.shape), "z", 0, 0)
    column = together(column.reshape(BLOCK, half))[0]
    parts = together(*[near(column, s) for s in (1, 2, 3)])
    (plane,) = together(jnp.concatenate([column, *parts], 0))
    two = far(plane, 2)
    one, three, peer, *state_out = together(
        far(plane, 1), far(plane, 3), swap(plane), *[state_out[k] for k in range(3)]
    )
    items = [(plane, 0, 0, 0), (one, 1, 0, 0), (three, 3, 0, 0), (peer, 0, 0, 1)]
    two, one_peer, three_peer, weight = together(two, swap(one), swap(three), join(here, items))
    items = [(two, 2, 0, 0), (one_peer, 1, 0, 1), (three_peer, 3, 0, 1)]
    two_peer, weight = together(swap(two), join(here, items, weight))
    weight = join(here, [(two_peer, 2, 0, 1)], weight)
    return (weight, state_out[0], state_out[1], state_out[2])


def solution(mesh):
    grid = Mesh(mesh.devices.reshape(SIZES), NAMES)
    rows = P(NAMES, None)
    in_specs = (rows, rows, rows, P(NAMES), P(NAMES), rows, rows, rows)
    out_specs = (P(), rows, rows, rows)
    return jax.shard_map(shards, mesh=grid, in_specs=in_specs, out_specs=out_specs, check_vma=False)
```

```python
import functools

import jax
import jax.numpy as jnp
from jax import lax
from jax.experimental import pallas as pl
from jax.experimental.pallas import tpu as pltpu
from jax.sharding import Mesh, PartitionSpec as P

STEP = 10

SIZES = (2, 4, 2, 8, 2)
NAMES = ("xlo", "y", "xhi", "z", "core")
N = 4
N_Z = 8
BLOCK = 64
SWAP = [(0, 1), (1, 0)]
VMEM = 40 * 1024 * 1024


def in_plane(value, shift, first_axis):
    def index(x, y, core):
        return (((x % 2) * N + y) * 2 + x // 2) * 2 + core

    pairs = []
    for x in range(N):
        for y in range(N):
            for core in range(2):
                if (core == 0) == first_axis:
                    there = index(x, y ^ shift, core)
                else:
                    there = index(x ^ shift, y, core)
                pairs.append((index(x, y, core), there))
    return lax.ppermute(value, ("xlo", "y", "xhi", "core"), pairs)


def far(value, shift):
    return in_plane(value, shift, True)


def near(value, shift):
    return in_plane(value, shift, False)


def swap(value):
    return lax.ppermute(value, "core", SWAP)


def block_row(here, core, far_step, near_step):
    dx = near_step + core * (far_step - near_step)
    dy = far_step + core * (near_step - far_step)
    x, y = here[0] ^ dx, here[1] ^ dy
    return pl.multiple_of(((x % 2) * 8 + y * 2 + x // 2) * BLOCK, BLOCK)


def terms_kernel(here, hidden, hidden_peer, scaled, scaled_peer, *refs):
    outs, turned = refs[:-1], refs[-1]
    tokens = hidden.shape[0]
    turned[:, :tokens] = hidden[...].T
    turned[:, tokens:] = hidden_peer[...].T
    columns = jnp.concatenate([scaled[...], scaled_peer[...]], 0)
    for f in range(N):
        rows = [turned[pl.ds(block_row(here, here[2], f, n), BLOCK), :] for n in range(N)]
        block = jnp.dot(jnp.concatenate(rows, 0), columns, preferred_element_type=jnp.float32)
        outs[f][...] = block[: 2 * BLOCK].astype(jnp.bfloat16)
        outs[N + f][...] = block[2 * BLOCK :].astype(jnp.bfloat16)


def terms(here, hidden, hidden_peer, scaled, scaled_peer):
    tokens, width = scaled.shape
    whole = pl.BlockSpec(memory_space=pltpu.VMEM)
    return pl.pallas_call(
        terms_kernel,
        out_shape=[jax.ShapeDtypeStruct((2 * BLOCK, width), jnp.bfloat16)] * (2 * N),
        in_specs=[pl.BlockSpec(memory_space=pltpu.SMEM)] + [whole] * 4,
        out_specs=[whole] * (2 * N),
        scratch_shapes=[pltpu.VMEM((hidden.shape[1], 2 * tokens), jnp.bfloat16)],
        compiler_params=pltpu.CompilerParams(vmem_limit_bytes=VMEM),
        cost_estimate=pl.CostEstimate(
            flops=2 * 2 * tokens * hidden.shape[1] * width,
            bytes_accessed=5_000_000,
            transcendentals=0,
        ),
    )(here, hidden, hidden_peer, scaled, scaled_peer)


def join_kernel(plan, here, *refs):
    pieces, out, sems = refs[: len(plan)], refs[-2], refs[-1]
    width = pieces[0].shape[1]
    copies = []
    for piece, (shift, begin, theirs) in zip(pieces, plan):
        core = 1 - here[2] if theirs else here[2]
        for n in range(piece.shape[0] // BLOCK):
            copy = pltpu.make_async_copy(
                piece.at[pl.ds(n * BLOCK, BLOCK), :],
                out.at[
                    pl.ds(block_row(here, core, shift, begin + n), BLOCK),
                    pl.ds(pl.multiple_of(core * width, 128), width),
                ],
                sems.at[len(copies)],
            )
            copy.start()
            copies.append(copy)
    for copy in copies:
        copy.wait()


def join(here, items, out=None):
    pieces = [item[0] for item in items]
    width = pieces[0].shape[1]
    blocks = sum(piece.shape[0] for piece in pieces) // BLOCK
    anywhere = pl.BlockSpec(memory_space=pl.ANY)
    begun = [] if out is None else [out]
    return pl.pallas_call(
        functools.partial(join_kernel, tuple(item[1:] for item in items)),
        out_shape=jax.ShapeDtypeStruct((N * N * BLOCK, 2 * width), jnp.bfloat16),
        in_specs=[pl.BlockSpec(memory_space=pltpu.SMEM)]
        + [pl.BlockSpec(memory_space=pltpu.VMEM)] * len(pieces)
        + [anywhere] * len(begun),
        out_specs=anywhere,
        scratch_shapes=[pltpu.SemaphoreType.DMA((blocks,))],
        input_output_aliases={len(pieces) + 1: 0} if begun else {},
        compiler_params=pltpu.CompilerParams(vmem_limit_bytes=VMEM),
        cost_estimate=pl.CostEstimate(
            flops=0, bytes_accessed=4 * blocks * BLOCK * width, transcendentals=0
        ),
    )(here, *pieces, *begun)


def together(*values):
    return lax.optimization_barrier(values)


def after(value, earlier):
    return lax.optimization_barrier((value, earlier))[0]


def total(parts):
    return functools.reduce(lambda a, b: a + b, [part.astype(jnp.float32) for part in parts])


def shards(gate_pre, up_pre, out_grad, route_weight, row_token, master, moment, second):
    core = lax.axis_index("core")
    first_core = core == 0
    here = jnp.stack([2 * lax.axis_index("xhi") + lax.axis_index("xlo"), lax.axis_index("y"), core])
    here = here.astype(jnp.int32)
    half = out_grad.shape[1] // 2

    def mine_and_theirs(whole):
        left, right = whole[..., :half], whole[..., half:]
        return jnp.where(first_core, left, right), jnp.where(first_core, right, left)

    def in_core_order(own, peer, axis):
        return jnp.where(
            first_core,
            jnp.concatenate([own, peer], axis),
            jnp.concatenate([peer, own], axis),
        )

    state = jnp.stack([master, moment, second])
    state_mine, state_theirs = mine_and_theirs(state)

    hidden = (jax.nn.silu(gate_pre.astype(jnp.float32)) * up_pre.astype(jnp.float32)).astype(
        jnp.bfloat16
    )
    named = row_token[:, None] == jnp.arange(out_grad.shape[0], dtype=jnp.int32)[None, :]
    picked = jnp.dot(named.astype(jnp.bfloat16), out_grad, preferred_element_type=jnp.float32)
    scaled = (picked * route_weight[:, None]).astype(jnp.bfloat16)
    scaled_mine, scaled_theirs = mine_and_theirs(scaled)

    blocks = terms(here, hidden, swap(hidden), scaled_mine, swap(scaled_theirs))
    tops, bottoms = blocks[:N], blocks[N:]
    from_one, from_three = far(bottoms[1], 1), far(tops[3], 3)
    over_three, over_one = together(far(tops[2], 3), far(bottoms[2], 1))
    to_one, to_three = together(
        total([tops[1], over_three]).astype(jnp.bfloat16),
        total([bottoms[3], over_one]).astype(jnp.bfloat16),
    )
    from_one, from_three, both_one, both_three, state_peer = together(
        from_one, from_three, far(to_one, 1), far(to_three, 3), swap(state_theirs)
    )
    state_chip = in_core_order(state_mine, state_peer, 1)
    halves = [[tops[0], both_one, from_three], [bottoms[0], from_one, both_three]]
    sums = [
        total([part[s % 2 * BLOCK : (s % 2 + 1) * BLOCK] for part in halves[s // 2]]) for s in range(N)
    ]
    sums = together(sums[0], *[sums[s].astype(jnp.bfloat16) for s in (2, 1, 3)])
    parts = [sums[0], *together(*[near(value, s) for value, s in zip(sums[1:], (2, 1, 3))])]
    plane_sum = total(parts).astype(jnp.bfloat16)
    parts = lax.all_to_all(plane_sum.reshape(N_Z, BLOCK // N_Z, half), "z", 0, 0)
    grad = jnp.sum(parts.astype(jnp.float32), 0)

    new_moment = 0.9 * state_chip[1] + 0.1 * grad
    new_second = 0.95 * state_chip[2] + 0.05 * grad * grad
    first_hat = new_moment / (1.0 - 0.9**STEP)
    second_hat = new_second / (1.0 - 0.95**STEP)
    new_master = state_chip[0] - 0.001 * (
        first_hat / (jnp.sqrt(second_hat) + 1e-08) + 0.1 * state_chip[0]
    )
    piece = new_master.astype(jnp.bfloat16)

    new_state = jnp.stack([new_master, new_moment, new_second])
    top, bottom = new_state[:, : master.shape[0]], new_state[:, master.shape[0] :]
    state_own = jnp.where(first_core, top, bottom)
    state_out = in_core_order(state_own, swap(jnp.where(first_core, bottom, top)), 2)

    column = lax.all_to_all(jnp.broadcast_to(piece, (N_Z,) + piece.shape), "z", 0, 0)
    column = together(column.reshape(BLOCK, half))[0]
    parts = together(*[near(column, s) for s in (1, 2, 3)])
    top, bottom = together(jnp.concatenate([column, parts[0]], 0), jnp.concatenate(parts[1:], 0))
    one_b, three_a = far(bottom, 1), far(top, 3)
    one_a, three_b, top_peer, *state_out = together(
        far(top, 1), far(bottom, 3), swap(top), *[state_out[k] for k in range(3)]
    )
    items = [(top, 0, 0, 0), (bottom, 0, 2, 0), (one_a, 1, 0, 0), (three_b, 3, 2, 0)]
    items += [(top_peer, 0, 0, 1)]
    one_b, three_a, two_a, two_b, bottom_peer, one_a, three_b, weight = together(
        one_b, three_a, far(one_a, 3), far(three_b, 1), swap(bottom), one_a, three_b, join(here, items)
    )
    items = [(one_b, 1, 2, 0), (three_a, 3, 0, 0), (two_a, 2, 0, 0), (two_b, 2, 2, 0)]
    items += [(bottom_peer, 0, 2, 1)]
    one_a, three_b, one_b, three_a, two_a, two_b, weight = together(
        *[swap(piece) for piece in (one_a, three_b, one_b, three_a)],
        two_a,
        two_b,
        join(here, items, weight),
    )
    items = [(one_a, 1, 0, 1), (three_b, 3, 2, 1), (one_b, 1, 2, 1), (three_a, 3, 0, 1)]
    two_a, two_b, weight = together(swap(two_a), swap(two_b), join(here, items, weight))
    weight = join(here, [(two_a, 2, 0, 1), (two_b, 2, 2, 1)], weight)
    return (weight, state_out[0], state_out[1], state_out[2])


def solution(mesh):
    grid = Mesh(mesh.devices.reshape(SIZES), NAMES)
    rows = P(NAMES, None)
    in_specs = (rows, rows, rows, P(NAMES), P(NAMES), rows, rows, rows)
    out_specs = (P(), rows, rows, rows)
    return jax.shard_map(shards, mesh=grid, in_specs=in_specs, out_specs=out_specs, check_vma=False)
```
